32 devices in a mesh: groups: 2 (over y), samp: 4 (over x, core), par: 4 (over z).
Axes of the slice: x: 2, y: 2, z: 4, core: 2. Of those that a mesh axis runs over, the one named last changes fastest.
Arguments:
- log_derivs: float32 [2048, 16384], P(('groups', 'samp'), 'par'), parts along dimension 0, may hold values from -20 to 20
Outputs:
- gram: float32 [2048, 1024], P(('groups', 'samp'), 'par'), parts along dimension 0
The draws below stay inside these ranges and needn't reach their ends.
There are 2 independent parts, one for each index of `groups`. The reference program is written for one: setup_inputs(seed, part) draws one part's arguments, and reference() takes and returns one part's arrays. A program takes and returns all parts, laid end to end along the dimension named above; each array names one. Nothing has to cross between parts.
All inputs are finite; a program needn't handle non-finite values.
Results may differ from the reference program's by a relative error of at most 0.00005.
Values sent between devices are 32-bit elements; how exact they have to be, the bound alone decides.
A program may use at most 64 MiB of HBM per device.

```python
import jax
import jax.numpy as jnp
from jax import lax

NP = 16384
NS = 1024


def draw_log_derivs(key, part):
    key = jax.random.fold_in(key, 11)
    keys = jax.random.split(key, 6)
    positions = jnp.arange(NS).astype(jnp.float32)
    ramp = 1.0 + 2.0 * positions / max(NS - 1, 1)
    weights = ramp * jax.random.uniform(keys[0], (NS,), jnp.float32, 0.6, 1.4)
    magnitude = jnp.exp(jax.random.uniform(keys[1], (NP,), jnp.float32, jnp.log(0.1), 0.0))
    signs = jnp.where(jax.random.bernoulli(keys[2], 0.5, (NP,)), 1.0, -1.0)
    offsets = magnitude * signs
    row_scale = jnp.exp(jax.random.uniform(keys[3], (NS, 1), jnp.float32, jnp.log(0.3), jnp.log(3.0)))
    col_scale = jnp.exp(jax.random.uniform(keys[4], (1, NP), jnp.float32, jnp.log(0.1), 0.0))
    noise = jax.random.truncated_normal(keys[5], -4.0, 4.0, (NS, NP), jnp.float32)
    noise_part = row_scale * col_scale * noise
    return (weights[:, None] * offsets[None, :] + noise_part).astype(jnp.float32)


def setup_inputs(seed: int = 0, part: int = 0) -> dict:
    splits = jax.random.split(jax.random.key(seed), 2)
    part_splits = jax.random.split(jax.random.fold_in(splits[1], part), 2)
    return {
        "log_derivs": draw_log_derivs(jax.random.fold_in(jax.random.fold_in(splits[1], part), 71), part),
    }


def reference(log_derivs):
    means = jnp.sum(log_derivs, axis=0) / NS
    centred = log_derivs - means[None, :]
    product = jnp.dot(centred, centred.T, precision=lax.Precision.HIGHEST, preferred_element_type=jnp.float32)
    return product / NS
```

```python
import functools

import jax
import jax.numpy as jnp
from jax import lax
from jax.experimental import pallas as pl
from jax.experimental.pallas import tpu as pltpu
from jax.sharding import PartitionSpec as P

MESH = pl.DeviceIdType.MESH


def split(value):
    high = value.astype(jnp.bfloat16)
    low = (value - high.astype(jnp.float32)).astype(jnp.bfloat16)
    return high, low


def dot_nt(a, b):
    return lax.dot_general(a, b, (((1,), (1,)), ((), ())), preferred_element_type=jnp.float32)


def dot_split(a_high, a_low, b_high, b_low):
    return dot_nt(a_high, b_high) + (dot_nt(a_high, b_low) + dot_nt(a_low, b_high))


def kernel(nsamp, npar, pieces, x_ref, out_ref, own, mate, raw, sums, mean, high, low, terms, arrived,
           total, mirrored, load_sem, sum_send, sum_recv, mate_send, mate_recv, raw_send, raw_recv,
           fwd_send, fwd_recv, z_send, z_recv, mir_send, mir_recv):
    rows, cols = own.shape
    half = cols // 2
    chips = nsamp // 2
    piece = rows // pieces
    total_rows = rows * nsamp
    items = (chips - 1) * pieces
    me = lax.axis_index("samp")
    z = lax.axis_index("par")
    chip = me // 2
    core = me % 2
    other = chip * 2 + (1 - core)
    block_chip = z // 2
    block_distance = (block_chip - chip + chips) % chips
    crosses = block_distance != 0

    load = pltpu.make_async_copy(x_ref, own, load_sem)
    load.start()

    barrier = pltpu.get_barrier_semaphore()
    for step in range(1, nsamp):
        pl.semaphore_signal(barrier, inc=1, device_id={"samp": (me + step) % nsamp}, device_id_type=MESH)
    for step in range(1, npar):
        pl.semaphore_signal(barrier, inc=1, device_id={"par": (z + step) % npar}, device_id_type=MESH)

    @pl.when(crosses)
    def _():
        pl.semaphore_signal(barrier, inc=1, device_id={"samp": z, "par": me}, device_id_type=MESH)

    pl.semaphore_wait(barrier, nsamp + npar - 2 + jnp.where(crosses, 1, 0))

    def piece_rows(k):
        return pl.ds(pl.multiple_of(k * piece, piece), piece)

    def raw_copy(d, k):
        there = (chip + d) % chips
        begin = pl.multiple_of(jnp.where(there < chip, 0, half), 128)
        slot = chips - 1 - d
        return pltpu.make_async_remote_copy(
            src_ref=x_ref.at[piece_rows(k), pl.ds(begin, half)],
            dst_ref=raw.at[slot, core, piece_rows(k)],
            send_sem=raw_send.at[d - 1, k],
            recv_sem=raw_recv.at[slot, k],
            device_id={"samp": there * 2 + core},
            device_id_type=MESH,
        )

    def raw_landed(d, k):
        return pltpu.make_async_remote_copy(
            src_ref=x_ref.at[piece_rows(k), pl.ds(0, half)],
            dst_ref=raw.at[d - 1, core, piece_rows(k)],
            send_sem=raw_send.at[d - 1, k],
            recv_sem=raw_recv.at[d - 1, k],
            device_id={"samp": other},
            device_id_type=MESH,
        )

    def fwd_copy(d, k, which):
        return pltpu.make_async_remote_copy(
            src_ref=raw.at[d - 1, which, piece_rows(k)],
            dst_ref=raw.at[d - 1, which, piece_rows(k)],
            send_sem=fwd_send.at[d - 1, k],
            recv_sem=fwd_recv.at[d - 1, k],
            device_id={"samp": other},
            device_id_type=MESH,
        )

    def sum_copy(source, target):
        return pltpu.make_async_remote_copy(
            src_ref=sums.at[source],
            dst_ref=sums.at[source],
            send_sem=sum_send.at[target],
            recv_sem=sum_recv.at[source],
            device_id={"samp": target},
            device_id_type=MESH,
        )

    mate_copy = pltpu.make_async_remote_copy(
        src_ref=x_ref,
        dst_ref=mate,
        send_sem=mate_send,
        recv_sem=mate_recv,
        device_id={"samp": other},
        device_id_type=MESH,
    )

    def z_copy(block, sender, target, where, k):
        return pltpu.make_async_remote_copy(
            src_ref=terms.at[block, where],
            dst_ref=arrived.at[sender, where],
            send_sem=z_send.at[block, k],
            recv_sem=z_recv.at[sender, k],
            device_id={"par": target},
            device_id_type=MESH,
        )

    def mirror_copy(k):
        return pltpu.make_async_remote_copy(
            src_ref=total.at[piece_rows(k)],
            dst_ref=mirrored.at[piece_rows(k)],
            send_sem=mir_send.at[k],
            recv_sem=mir_recv.at[k],
            device_id={"samp": z, "par": me},
            device_id_type=MESH,
        )

    everything = pl.ds(0, rows)

    for d in range(1, chips):
        raw_copy(d, 0).start()
    load.wait()

    def add_rows(i, acc):
        return acc + own[pl.ds(pl.multiple_of(i * 8, 8), 8), :]

    acc = lax.fori_loop(1, rows // 8, add_rows, own[pl.ds(0, 8), :])
    sums[me] = jnp.sum(acc, axis=0, keepdims=True)
    for step in range(1, nsamp):
        sum_copy(me, (me + step) % nsamp).start()
    mate_copy.start()

    @pl.loop(0, chips - 1)
    def _(i):
        @pl.loop(1, pieces)
        def _(k):
            raw_copy(i + 1, k).start()

    for step in range(1, nsamp):
        sum_copy((me + step) % nsamp, me).wait_recv()
    col_sum = sums[0]
    for s in range(1, nsamp):
        col_sum = col_sum + sums[s]
    mean[...] = col_sum / total_rows

    @pl.loop(0, rows // 16)
    def _(i):
        at = pl.ds(pl.multiple_of(i * 16, 16), 16)
        h, l = split(own[at, :] - mean[...])
        high[at, :] = h
        low[at, :] = l

    width = min(512, cols)

    def send_block(block, where, k):
        @pl.when(block != z)
        def _():
            z_copy(block, z, block, where, k).start()

        @pl.when(block == z)
        def _():
            arrived[z, where] = terms[block, where]

    terms[me] = jnp.zeros((rows, rows), jnp.float32)

    @pl.loop(0, cols // width)
    def _(i):
        at = pl.ds(pl.multiple_of(i * width, width), width)
        h = high[:, at]
        l = low[:, at]
        terms[me] += dot_split(h, l, h, l)

    send_block(me, everything, 0)
    terms[other] = jnp.zeros((rows, rows), jnp.float32)
    mate_copy.wait_recv()

    @pl.loop(0, cols // width)
    def _(i):
        at = pl.ds(pl.multiple_of(i * width, width), width)
        h, l = split(mate[:, at] - mean[:, at])
        terms[other] += dot_split(h, l, high[:, at], low[:, at])

    send_block(other, everything, 0)

    def chunk_term(d, k, which):
        there = (chip + d) % chips
        begin = pl.multiple_of(jnp.where(chip < there, 0, half), 128)
        at = pl.ds(begin, half)
        h, l = split(raw[d - 1, which, piece_rows(k)] - mean[:, at])
        block = there * 2 + which
        terms[block, piece_rows(k)] = dot_split(h, l, high[:, at], low[:, at])
        send_block(block, piece_rows(k), k)

    def gather_sum(k):
        where = piece_rows(k)
        for step in range(1, npar):
            z_copy(z, (z + step) % npar, z, where, k).wait_recv()
        value = arrived[0, where]
        for s in range(1, npar):
            value = value + arrived[s, where]
        total[where] = value
        mirror_copy(k).start()

    def gather_item(j):
        @pl.when(crosses & (j // pieces + 1 == block_distance))
        def _():
            gather_sum(j % pieces)

    @pl.loop(0, items)
    def _(j):
        d = j // pieces + 1
        k = j % pieces
        raw_landed(d, k).wait_recv()
        fwd_copy(d, k, core).start()
        chunk_term(d, k, core)
        fwd_copy(d, k, 1 - core).wait_recv()
        chunk_term(d, k, 1 - core)

        @pl.when(j > 0)
        def _():
            gather_item(j - 1)

    gather_item(items - 1)

    @pl.when(jnp.logical_not(crosses))
    def _():
        for step in range(1, npar):
            z_copy(z, (z + step) % npar, z, everything, 0).wait_recv()
        value = arrived[0]
        for s in range(1, npar):
            value = value + arrived[s]
        out_ref[...] = value.T / total_rows

    @pl.when(crosses)
    def _():
        flipped = total[...].T

        @pl.loop(0, pieces)
        def _(k):
            mirror_copy(k).wait_recv()

        out_ref[...] = (flipped + mirrored[...]) / total_rows

        @pl.loop(0, pieces)
        def _(k):
            mirror_copy(k).wait_send()

    for step in range(1, nsamp):
        sum_copy(me, (me + step) % nsamp).wait_send()
    mate_copy.wait_send()

    @pl.loop(0, items)
    def _(j):
        d = j // pieces + 1
        k = j % pieces
        raw_copy(d, k).wait_send()
        fwd_copy(d, k, core).wait_send()
        for which in range(2):
            block = ((chip + d) % chips) * 2 + which

            @pl.when(block != z)
            def _():
                z_copy(block, z, block, piece_rows(k), k).wait_send()

    for block in (me, other):
        @pl.when(block != z)
        def _():
            z_copy(block, z, block, everything, 0).wait_send()


def per_device(nsamp, npar, log_derivs):
    rows, cols = log_derivs.shape
    pieces = 8
    chips = nsamp // 2
    dma = pltpu.SemaphoreType.DMA
    f32, bf16 = jnp.float32, jnp.bfloat16
    return pl.pallas_call(
        functools.partial(kernel, nsamp, npar, pieces),
        out_shape=jax.ShapeDtypeStruct((rows, rows), f32),
        in_specs=[pl.BlockSpec(memory_space=pl.ANY)],
        out_specs=pl.BlockSpec(memory_space=pltpu.VMEM),
        scratch_shapes=[
            pltpu.VMEM((rows, cols), f32),
            pltpu.VMEM((rows, cols), f32),
            pltpu.VMEM((chips - 1, 2, rows, cols // 2), f32),
            pltpu.VMEM((nsamp, 1, cols), f32),
            pltpu.VMEM((1, cols), f32),
            pltpu.VMEM((rows, cols), bf16),
            pltpu.VMEM((rows, cols), bf16),
            pltpu.VMEM((nsamp, rows, rows), f32),
            pltpu.VMEM((npar, rows, rows), f32),
            pltpu.VMEM((rows, rows), f32),
            pltpu.VMEM((rows, rows), f32),
            dma,
            dma((nsamp,)),
            dma((nsamp,)),
            dma,
            dma,
            dma((chips - 1, pieces)),
            dma((chips - 1, pieces)),
            dma((chips - 1, pieces)),
            dma((chips - 1, pieces)),
            dma((nsamp, pieces)),
            dma((npar, pieces)),
            dma((pieces,)),
            dma((pieces,)),
        ],
        compiler_params=pltpu.CompilerParams(
            collective_id=0, has_side_effects=True, vmem_limit_bytes=48 * 1024 * 1024
        ),
    )(log_derivs)


def solution(mesh):
    nsamp, npar = mesh.shape["samp"], mesh.shape["par"]
    spec = P(("groups", "samp"), "par")
    return jax.shard_map(
        functools.partial(per_device, nsamp, npar),
        mesh=mesh, in_specs=(spec,), out_specs=spec, check_vma=False,
    )
```

```python
import functools

import jax
import jax.numpy as jnp
from jax import lax
from jax.experimental import pallas as pl
from jax.experimental.pallas import tpu as pltpu
from jax.sharding import PartitionSpec as P

MESH = pl.DeviceIdType.MESH
FLIP = False


def split(value):
    high = value.astype(jnp.bfloat16)
    low = (value - high.astype(jnp.float32)).astype(jnp.bfloat16)
    return high, low


def dot_nt(a, b):
    return lax.dot_general(a, b, (((1,), (1,)), ((), ())), preferred_element_type=jnp.float32)


def dot_split(a_high, a_low, b_high, b_low):
    return dot_nt(a_high, b_high) + (dot_nt(a_high, b_low) + dot_nt(a_low, b_high))


def kernel(nsamp, npar, sizes, x_ref, out_ref, own, mate, raw, middle, sums, mean, high, low, terms, arrived,
           total, mirrored, load_sem, sum_send, sum_recv, mate_send, mate_recv, raw_send, raw_recv,
           fwd_send, fwd_recv, mid_send, mid_recv, midfwd_send, midfwd_recv, z_send, z_recv, mir_send, mir_recv):
    rows, cols = own.shape
    span = raw.shape[3]
    spare = cols - 2 * span
    chips = nsamp // 2
    pieces = len(sizes)
    starts = [sum(sizes[:k]) for k in range(pieces)]
    total_rows = rows * nsamp
    me = lax.axis_index("samp")
    z = lax.axis_index("par")
    chip = me // 2
    core = me % 2
    other = chip * 2 + (1 - core)
    block_chip = z // 2
    block_distance = (block_chip - chip + chips) % chips
    crosses = block_distance != 0

    load = pltpu.make_async_copy(x_ref, own, load_sem)
    load.start()

    barrier = pltpu.get_barrier_semaphore()
    for step in range(1, nsamp):
        pl.semaphore_signal(barrier, inc=1, device_id={"samp": (me + step) % nsamp}, device_id_type=MESH)
    for step in range(1, npar):
        pl.semaphore_signal(barrier, inc=1, device_id={"par": (z + step) % npar}, device_id_type=MESH)

    @pl.when(crosses)
    def _():
        pl.semaphore_signal(barrier, inc=1, device_id={"samp": z, "par": me}, device_id_type=MESH)

    pl.semaphore_wait(barrier, nsamp + npar - 2 + jnp.where(crosses, 1, 0))

    def piece_rows(k):
        return pl.ds(starts[k], sizes[k])

    def lower_takes_middle(low_chip, high_chip):
        return (z // 2 != low_chip) if FLIP else (z // 2 == low_chip)

    def takes_middle(taker, giver):
        lower = jnp.minimum(taker, giver)
        return lower_takes_middle(lower, jnp.maximum(taker, giver)) == (taker == lower)

    def raw_copy(d, k):
        there = (chip + d) % chips
        begin = pl.multiple_of(jnp.where(there < chip, 0, cols - span), 128)
        slot = chips - 1 - d
        return pltpu.make_async_remote_copy(
            src_ref=x_ref.at[piece_rows(k), pl.ds(begin, span)],
            dst_ref=raw.at[slot, core, piece_rows(k)],
            send_sem=raw_send.at[d - 1, k],
            recv_sem=raw_recv.at[slot, k],
            device_id={"samp": there * 2 + core},
            device_id_type=MESH,
        )

    def raw_landed(d, k):
        return pltpu.make_async_remote_copy(
            src_ref=x_ref.at[piece_rows(k), pl.ds(0, span)],
            dst_ref=raw.at[d - 1, core, piece_rows(k)],
            send_sem=raw_send.at[d - 1, k],
            recv_sem=raw_recv.at[d - 1, k],
            device_id={"samp": other},
            device_id_type=MESH,
        )

    def fwd_copy(d, k, which):
        return pltpu.make_async_remote_copy(
            src_ref=raw.at[d - 1, which, piece_rows(k)],
            dst_ref=raw.at[d - 1, which, piece_rows(k)],
            send_sem=fwd_send.at[d - 1, k],
            recv_sem=fwd_recv.at[d - 1, k],
            device_id={"samp": other},
            device_id_type=MESH,
        )

    def mid_copy(d):
        there = (chip + d) % chips
        slot = chips - 1 - d
        return pltpu.make_async_remote_copy(
            src_ref=x_ref.at[:, pl.ds(span, spare)],
            dst_ref=middle.at[slot, core],
            send_sem=mid_send.at[d - 1],
            recv_sem=mid_recv.at[slot],
            device_id={"samp": there * 2 + core},
            device_id_type=MESH,
        )

    def mid_landed(d):
        return pltpu.make_async_remote_copy(
            src_ref=x_ref.at[:, pl.ds(span, spare)],
            dst_ref=middle.at[d - 1, core],
            send_sem=mid_send.at[d - 1],
            recv_sem=mid_recv.at[d - 1],
            device_id={"samp": other},
            device_id_type=MESH,
        )

    def midfwd_copy(d, which):
        return pltpu.make_async_remote_copy(
            src_ref=middle.at[d - 1, which],
            dst_ref=middle.at[d - 1, which],
            send_sem=midfwd_send.at[d - 1],
            recv_sem=midfwd_recv.at[d - 1],
            device_id={"samp": other},
            device_id_type=MESH,
        )

    def sum_copy(source, target):
        return pltpu.make_async_remote_copy(
            src_ref=sums.at[source],
            dst_ref=sums.at[source],
            send_sem=sum_send.at[target],
            recv_sem=sum_recv.at[source],
            device_id={"samp": target},
            device_id_type=MESH,
        )

    mate_copy = pltpu.make_async_remote_copy(
        src_ref=x_ref,
        dst_ref=mate,
        send_sem=mate_send,
        recv_sem=mate_recv,
        device_id={"samp": other},
        device_id_type=MESH,
    )

    def z_copy(block, sender, target, where, k):
        return pltpu.make_async_remote_copy(
            src_ref=terms.at[block, where],
            dst_ref=arrived.at[sender, where],
            send_sem=z_send.at[block, k],
            recv_sem=z_recv.at[sender, k],
            device_id={"par": target},
            device_id_type=MESH,
        )

    def mirror_copy(k):
        return pltpu.make_async_remote_copy(
            src_ref=total.at[piece_rows(k)],
            dst_ref=mirrored.at[piece_rows(k)],
            send_sem=mir_send.at[k],
            recv_sem=mir_recv.at[k],
            device_id={"samp": z, "par": me},
            device_id_type=MESH,
        )

    everything = pl.ds(0, rows)

    for d in range(1, chips):
        @pl.when(takes_middle((chip + d) % chips, chip))
        def _():
            mid_copy(d).start()

        raw_copy(d, 0).start()
    load.wait()

    def add_rows(i, acc):
        return acc + own[pl.ds(pl.multiple_of(i * 8, 8), 8), :]

    acc = lax.fori_loop(1, rows // 8, add_rows, own[pl.ds(0, 8), :])
    sums[me] = jnp.sum(acc, axis=0, keepdims=True)
    for step in range(1, nsamp):
        sum_copy(me, (me + step) % nsamp).start()
    mate_copy.start()

    @pl.loop(1, chips)
    def _(d):
        for k in range(1, pieces):
            raw_copy(d, k).start()

    for step in range(1, nsamp):
        sum_copy((me + step) % nsamp, me).wait_recv()
    col_sum = sums[0]
    for s in range(1, nsamp):
        col_sum = col_sum + sums[s]
    mean[...] = col_sum / total_rows

    @pl.loop(0, rows // 16)
    def _(i):
        at = pl.ds(pl.multiple_of(i * 16, 16), 16)
        h, l = split(own[at, :] - mean[...])
        high[at, :] = h
        low[at, :] = l

    width = min(512, cols)

    def send_block(block, where, k):
        @pl.when(block != z)
        def _():
            z_copy(block, z, block, where, k).start()

        @pl.when(block == z)
        def _():
            arrived[z, where] = terms[block, where]

    terms[me] = jnp.zeros((rows, rows), jnp.float32)

    @pl.loop(0, cols // width)
    def _(i):
        at = pl.ds(pl.multiple_of(i * width, width), width)
        h = high[:, at]
        l = low[:, at]
        terms[me] += dot_split(h, l, h, l)

    send_block(me, everything, 0)
    terms[other] = jnp.zeros((rows, rows), jnp.float32)
    mate_copy.wait_recv()

    @pl.loop(0, cols // width)
    def _(i):
        at = pl.ds(pl.multiple_of(i * width, width), width)
        h, l = split(mate[:, at] - mean[:, at])
        terms[other] += dot_split(h, l, high[:, at], low[:, at])

    send_block(other, everything, 0)

    def first_terms(d):
        there = (chip + d) % chips
        takes = takes_middle(chip, there)

        @pl.when(takes)
        def _():
            at = pl.ds(span, spare)
            mid_landed(d).wait_recv()
            midfwd_copy(d, core).start()
            midfwd_copy(d, 1 - core).wait_recv()
            for which in range(2):
                h, l = split(middle[d - 1, which] - mean[:, at])
                terms[there * 2 + which] = dot_split(h, l, high[:, at], low[:, at])

        @pl.when(jnp.logical_not(takes))
        def _():
            for which in range(2):
                terms[there * 2 + which] = jnp.zeros((rows, rows), jnp.float32)

    def chunk_terms(d, k):
        there = (chip + d) % chips
        begin = pl.multiple_of(jnp.where(chip < there, 0, cols - span), 128)
        at = pl.ds(begin, span)
        where = piece_rows(k)
        size = sizes[k]
        both = jnp.concatenate([raw[d - 1, 0, where], raw[d - 1, 1, where]], axis=0) - mean[:, at]
        h, l = split(both)
        stacked = dot_nt(jnp.concatenate([h, l], axis=0), high[:, at])
        value = stacked[:2 * size] + (stacked[2 * size:] + dot_nt(h, low[:, at]))
        for which in range(2):
            block = there * 2 + which
            terms[block, where] += value[which * size:(which + 1) * size]
            send_block(block, where, k)

    def gather_sum(k):
        where = piece_rows(k)
        for step in range(1, npar):
            z_copy(z, (z + step) % npar, z, where, k).wait_recv()
        value = arrived[0, where]
        for s in range(1, npar):
            value = value + arrived[s, where]
        total[where] = value
        mirror_copy(k).start()

    def gather_piece(d, k):
        @pl.when(block_distance == d)
        def _():
            gather_sum(k)

    @pl.loop(1, chips)
    def _(d):
        first_terms(d)
        for k in range(pieces):
            raw_landed(d, k).wait_recv()
            fwd_copy(d, k, core).start()
            fwd_copy(d, k, 1 - core).wait_recv()
            chunk_terms(d, k)
            if k > 0:
                gather_piece(d, k - 1)
        gather_piece(d, pieces - 1)

    @pl.when(jnp.logical_not(crosses))
    def _():
        for step in range(1, npar):
            z_copy(z, (z + step) % npar, z, everything, 0).wait_recv()
        value = arrived[0]
        for s in range(1, npar):
            value = value + arrived[s]
        out_ref[...] = value.T / total_rows

    @pl.when(crosses)
    def _():
        flipped = total[...].T

        for k in range(pieces):
            mirror_copy(k).wait_recv()
            where = piece_rows(k)
            out_ref[where] = (flipped[starts[k]:starts[k] + sizes[k]] + mirrored[where]) / total_rows
        for k in range(pieces):
            mirror_copy(k).wait_send()

    for step in range(1, nsamp):
        sum_copy(me, (me + step) % nsamp).wait_send()
    mate_copy.wait_send()

    @pl.loop(1, chips)
    def _(d):
        there = (chip + d) % chips

        @pl.when(takes_middle(there, chip))
        def _():
            mid_copy(d).wait_send()

        @pl.when(takes_middle(chip, there))
        def _():
            midfwd_copy(d, core).wait_send()

        for k in range(pieces):
            raw_copy(d, k).wait_send()
            fwd_copy(d, k, core).wait_send()
            for which in range(2):
                block = there * 2 + which

                @pl.when(block != z)
                def _():
                    z_copy(block, z, block, piece_rows(k), k).wait_send()

    for block in (me, other):
        @pl.when(block != z)
        def _():
            z_copy(block, z, block, everything, 0).wait_send()


def piece_sizes(rows):
    sizes = [64] * (rows // 64 - 1) + [32]
    return sizes + [16, 16]


def per_device(nsamp, npar, log_derivs):
    rows, cols = log_derivs.shape
    sizes = piece_sizes(rows)
    pieces = len(sizes)
    spare = 256
    span = (cols - spare) // 2
    chips = nsamp // 2
    dma = pltpu.SemaphoreType.DMA
    f32, bf16 = jnp.float32, jnp.bfloat16
    return pl.pallas_call(
        functools.partial(kernel, nsamp, npar, sizes),
        out_shape=jax.ShapeDtypeStruct((rows, rows), f32),
        in_specs=[pl.BlockSpec(memory_space=pltpu.HBM)],
        out_specs=pl.BlockSpec(memory_space=pltpu.VMEM),
        scratch_shapes=[
            pltpu.VMEM((rows, cols), f32),
            pltpu.VMEM((rows, cols), f32),
            pltpu.VMEM((chips - 1, 2, rows, span), f32),
            pltpu.VMEM((chips - 1, 2, rows, spare), f32),
            pltpu.VMEM((nsamp, 1, cols), f32),
            pltpu.VMEM((1, cols), f32),
            pltpu.VMEM((rows, cols), bf16),
            pltpu.VMEM((rows, cols), bf16),
            pltpu.VMEM((nsamp, rows, rows), f32),
            pltpu.VMEM((npar, rows, rows), f32),
            pltpu.VMEM((rows, rows), f32),
            pltpu.VMEM((rows, rows), f32),
            dma,
            dma((nsamp,)),
            dma((nsamp,)),
            dma,
            dma,
            dma((chips - 1, pieces)),
            dma((chips - 1, pieces)),
            dma((chips - 1, pieces)),
            dma((chips - 1, pieces)),
            dma((chips - 1,)),
            dma((chips - 1,)),
            dma((chips - 1,)),
            dma((chips - 1,)),
            dma((nsamp, pieces)),
            dma((npar, pieces)),
            dma((pieces,)),
            dma((pieces,)),
        ],
        compiler_params=pltpu.CompilerParams(
            collective_id=0, has_side_effects=True, vmem_limit_bytes=48 * 1024 * 1024
        ),
    )(log_derivs)


def solution(mesh):
    nsamp, npar = mesh.shape["samp"], mesh.shape["par"]
    spec = P(("groups", "samp"), "par")
    return jax.shard_map(
        functools.partial(per_device, nsamp, npar),
        mesh=mesh, in_specs=(spec,), out_specs=spec, check_vma=False,
    )
```

```python
import functools

import jax
import jax.numpy as jnp
from jax import lax
from jax.experimental import pallas as pl
from jax.experimental.pallas import tpu as pltpu
from jax.sharding import PartitionSpec as P

MESH = pl.DeviceIdType.MESH


def split(value):
    high = value.astype(jnp.bfloat16)
    low = (value - high.astype(jnp.float32)).astype(jnp.bfloat16)
    return high, low


def dot_nt(a, b):
    return lax.dot_general(a, b, (((1,), (1,)), ((), ())), preferred_element_type=jnp.float32)


def dot_split(a_high, a_low, b_high, b_low):
    return dot_nt(a_high, b_high) + (dot_nt(a_high, b_low) + dot_nt(a_low, b_high))


def kernel(nsamp, npar, pieces, x_ref, out_ref, own, mate, raw, sums, mean, high, low, terms, arrived,
           total, mirrored, load_sem, sum_send, sum_recv, mate_send, mate_recv, raw_send, raw_recv,
           fwd_send, fwd_recv, z_send, z_recv, mir_send, mir_recv):
    rows, cols = own.shape
    half = cols // 2
    chips = nsamp // 2
    piece = rows // pieces
    total_rows = rows * nsamp
    items = (chips - 1) * pieces
    me = lax.axis_index("samp")
    z = lax.axis_index("par")
    chip = me // 2
    core = me % 2
    other = chip * 2 + (1 - core)
    block_chip = z // 2
    block_distance = (block_chip - chip + chips) % chips
    crosses = block_distance != 0

    load = pltpu.make_async_copy(x_ref, own, load_sem)
    load.start()

    barrier = pltpu.get_barrier_semaphore()
    for step in range(1, nsamp):
        pl.semaphore_signal(barrier, inc=1, device_id={"samp": (me + step) % nsamp}, device_id_type=MESH)
    for step in range(1, npar):
        pl.semaphore_signal(barrier, inc=1, device_id={"par": (z + step) % npar}, device_id_type=MESH)

    @pl.when(crosses)
    def _():
        pl.semaphore_signal(barrier, inc=1, device_id={"samp": z, "par": me}, device_id_type=MESH)

    pl.semaphore_wait(barrier, nsamp + npar - 2 + jnp.where(crosses, 1, 0))

    def piece_rows(k):
        return pl.ds(pl.multiple_of(k * piece, piece), piece)

    def raw_copy(d, k):
        there = (chip + d) % chips
        begin = pl.multiple_of(jnp.where(there < chip, 0, half), 128)
        slot = chips - 1 - d
        return pltpu.make_async_remote_copy(
            src_ref=x_ref.at[piece_rows(k), pl.ds(begin, half)],
            dst_ref=raw.at[slot, core, piece_rows(k)],
            send_sem=raw_send.at[d - 1, k],
            recv_sem=raw_recv.at[slot, k],
            device_id={"samp": there * 2 + core},
            device_id_type=MESH,
        )

    def raw_landed(d, k):
        return pltpu.make_async_remote_copy(
            src_ref=x_ref.at[piece_rows(k), pl.ds(0, half)],
            dst_ref=raw.at[d - 1, core, piece_rows(k)],
            send_sem=raw_send.at[d - 1, k],
            recv_sem=raw_recv.at[d - 1, k],
            device_id={"samp": other},
            device_id_type=MESH,
        )

    def fwd_copy(d, k, which):
        return pltpu.make_async_remote_copy(
            src_ref=raw.at[d - 1, which, piece_rows(k)],
            dst_ref=raw.at[d - 1, which, piece_rows(k)],
            send_sem=fwd_send.at[d - 1, k],
            recv_sem=fwd_recv.at[d - 1, k],
            device_id={"samp": other},
            device_id_type=MESH,
        )

    def sum_copy(source, target):
        return pltpu.make_async_remote_copy(
            src_ref=sums.at[source],
            dst_ref=sums.at[source],
            send_sem=sum_send.at[target],
            recv_sem=sum_recv.at[source],
            device_id={"samp": target},
            device_id_type=MESH,
        )

    mate_copy = pltpu.make_async_remote_copy(
        src_ref=x_ref,
        dst_ref=mate,
        send_sem=mate_send,
        recv_sem=mate_recv,
        device_id={"samp": other},
        device_id_type=MESH,
    )

    def z_copy(block, sender, target, where, k):
        return pltpu.make_async_remote_copy(
            src_ref=terms.at[block, where],
            dst_ref=arrived.at[sender, where],
            send_sem=z_send.at[block, k],
            recv_sem=z_recv.at[sender, k],
            device_id={"par": target},
            device_id_type=MESH,
        )

    def mirror_copy(k):
        return pltpu.make_async_remote_copy(
            src_ref=total.at[piece_rows(k)],
            dst_ref=mirrored.at[piece_rows(k)],
            send_sem=mir_send.at[k],
            recv_sem=mir_recv.at[k],
            device_id={"samp": z, "par": me},
            device_id_type=MESH,
        )

    everything = pl.ds(0, rows)

    for d in range(1, chips):
        raw_copy(d, 0).start()
    load.wait()

    def add_rows(i, acc):
        return acc + own[pl.ds(pl.multiple_of(i * 8, 8), 8), :]

    acc = lax.fori_loop(1, rows // 8, add_rows, own[pl.ds(0, 8), :])
    sums[me] = jnp.sum(acc, axis=0, keepdims=True)
    for step in range(1, nsamp):
        sum_copy(me, (me + step) % nsamp).start()
    mate_copy.start()

    @pl.loop(0, chips - 1)
    def _(i):
        @pl.loop(1, pieces)
        def _(k):
            raw_copy(i + 1, k).start()

    for step in range(1, nsamp):
        sum_copy((me + step) % nsamp, me).wait_recv()
    col_sum = sums[0]
    for s in range(1, nsamp):
        col_sum = col_sum + sums[s]
    mean[...] = col_sum / total_rows

    @pl.loop(0, rows // 16)
    def _(i):
        at = pl.ds(pl.multiple_of(i * 16, 16), 16)
        h, l = split(own[at, :] - mean[...])
        high[at, :] = h
        low[at, :] = l

    width = min(512, cols)

    def send_block(block, where, k):
        @pl.when(block != z)
        def _():
            z_copy(block, z, block, where, k).start()

        @pl.when(block == z)
        def _():
            arrived[z, where] = terms[block, where]

    terms[me] = jnp.zeros((rows, rows), jnp.float32)

    @pl.loop(0, cols // width)
    def _(i):
        at = pl.ds(pl.multiple_of(i * width, width), width)
        h = high[:, at]
        l = low[:, at]
        terms[me] += dot_split(h, l, h, l)

    send_block(me, everything, 0)
    terms[other] = jnp.zeros((rows, rows), jnp.float32)
    mate_copy.wait_recv()

    @pl.loop(0, cols // width)
    def _(i):
        at = pl.ds(pl.multiple_of(i * width, width), width)
        h, l = split(mate[:, at] - mean[:, at])
        terms[other] += dot_split(h, l, high[:, at], low[:, at])

    send_block(other, everything, 0)

    def chunk_term(d, k, which):
        there = (chip + d) % chips
        begin = pl.multiple_of(jnp.where(chip < there, 0, half), 128)
        at = pl.ds(begin, half)
        h, l = split(raw[d - 1, which, piece_rows(k)] - mean[:, at])
        block = there * 2 + which
        stacked = dot_nt(jnp.concatenate([h, l], axis=0), high[:, at])
        terms[block, piece_rows(k)] = stacked[:piece] + (stacked[piece:] + dot_nt(h, low[:, at]))
        send_block(block, piece_rows(k), k)

    def gather_sum(k):
        where = piece_rows(k)
        for step in range(1, npar):
            z_copy(z, (z + step) % npar, z, where, k).wait_recv()
        value = arrived[0, where]
        for s in range(1, npar):
            value = value + arrived[s, where]
        total[where] = value
        mirror_copy(k).start()

    def gather_item(j):
        @pl.when(crosses & (j // pieces + 1 == block_distance))
        def _():
            gather_sum(j % pieces)

    @pl.loop(0, items)
    def _(j):
        d = j // pieces + 1
        k = j % pieces
        raw_landed(d, k).wait_recv()
        fwd_copy(d, k, core).start()
        chunk_term(d, k, core)
        fwd_copy(d, k, 1 - core).wait_recv()
        chunk_term(d, k, 1 - core)

        @pl.when(j > 0)
        def _():
            gather_item(j - 1)

    gather_item(items - 1)

    @pl.when(jnp.logical_not(crosses))
    def _():
        for step in range(1, npar):
            z_copy(z, (z + step) % npar, z, everything, 0).wait_recv()
        value = arrived[0]
        for s in range(1, npar):
            value = value + arrived[s]
        out_ref[...] = value.T / total_rows

    @pl.when(crosses)
    def _():
        flipped = total[...].T

        @pl.loop(0, pieces)
        def _(k):
            mirror_copy(k).wait_recv()

        out_ref[...] = (flipped + mirrored[...]) / total_rows

        @pl.loop(0, pieces)
        def _(k):
            mirror_copy(k).wait_send()

    for step in range(1, nsamp):
        sum_copy(me, (me + step) % nsamp).wait_send()
    mate_copy.wait_send()

    @pl.loop(0, items)
    def _(j):
        d = j // pieces + 1
        k = j % pieces
        raw_copy(d, k).wait_send()
        fwd_copy(d, k, core).wait_send()
        for which in range(2):
            block = ((chip + d) % chips) * 2 + which

            @pl.when(block != z)
            def _():
                z_copy(block, z, block, piece_rows(k), k).wait_send()

    for block in (me, other):
        @pl.when(block != z)
        def _():
            z_copy(block, z, block, everything, 0).wait_send()


def per_device(nsamp, npar, log_derivs):
    rows, cols = log_derivs.shape
    pieces = 8
    chips = nsamp // 2
    dma = pltpu.SemaphoreType.DMA
    f32, bf16 = jnp.float32, jnp.bfloat16
    return pl.pallas_call(
        functools.partial(kernel, nsamp, npar, pieces),
        out_shape=jax.ShapeDtypeStruct((rows, rows), f32),
        in_specs=[pl.BlockSpec(memory_space=pltpu.HBM)],
        out_specs=pl.BlockSpec(memory_space=pltpu.VMEM),
        scratch_shapes=[
            pltpu.VMEM((rows, cols), f32),
            pltpu.VMEM((rows, cols), f32),
            pltpu.VMEM((chips - 1, 2, rows, cols // 2), f32),
            pltpu.VMEM((nsamp, 1, cols), f32),
            pltpu.VMEM((1, cols), f32),
            pltpu.VMEM((rows, cols), bf16),
            pltpu.VMEM((rows, cols), bf16),
            pltpu.VMEM((nsamp, rows, rows), f32),
            pltpu.VMEM((npar, rows, rows), f32),
            pltpu.VMEM((rows, rows), f32),
            pltpu.VMEM((rows, rows), f32),
            dma,
            dma((nsamp,)),
            dma((nsamp,)),
            dma,
            dma,
            dma((chips - 1, pieces)),
            dma((chips - 1, pieces)),
            dma((chips - 1, pieces)),
            dma((chips - 1, pieces)),
            dma((nsamp, pieces)),
            dma((npar, pieces)),
            dma((pieces,)),
            dma((pieces,)),
        ],
        compiler_params=pltpu.CompilerParams(
            collective_id=0, has_side_effects=True, vmem_limit_bytes=48 * 1024 * 1024
        ),
    )(log_derivs)


def solution(mesh):
    nsamp, npar = mesh.shape["samp"], mesh.shape["par"]
    spec = P(("groups", "samp"), "par")
    return jax.shard_map(
        functools.partial(per_device, nsamp, npar),
        mesh=mesh, in_specs=(spec,), out_specs=spec, check_vma=False,
    )
```
